32 devices in a mesh: groups: 2 (over x), expert: 16 (over z, y, core).
Axes of the slice: x: 2, y: 2, z: 4, core: 2. Of those that a mesh axis runs over, the one named last changes fastest.
Arguments:
- tokens: bfloat16 [2, 2048, 2048], P(None, ('groups', 'expert')), parts along dimension 1, may hold values from -6 to 6
- w_gate: bfloat16 [16, 2048, 768], P('expert'), may hold values from -0.125 to 0.125
- w_up: bfloat16 [16, 2048, 768], P('expert'), may hold values from -0.125 to 0.125
- w_down: bfloat16 [16, 768, 2048], P('expert'), may hold values from -0.21875 to 0.21875
- hot_gate: bfloat16 [2, 2048, 768], P(None, None, 'expert'), may hold values from -0.125 to 0.125
- hot_up: bfloat16 [2, 2048, 768], P(None, None, 'expert'), may hold values from -0.125 to 0.125
- hot_down: bfloat16 [2, 2048, 768], P(None, None, 'expert'), may hold values from -0.21875 to 0.21875
- cold_routes: int32 [2, 2048, 7], P(None, ('groups', 'expert')), parts along dimension 1, may hold values from 0 to 15, all different within a row; in each aligned block of 64 rows (0 to 63, 64 to 127, ..., all dimensions but the last counted through in order) at most 43 rows name the same one
- hot_pick: int32 [2, 2048], P(None, ('groups', 'expert')), parts along dimension 1, may hold values from 0 to 1, as said below
- gates: float32 [2, 2048, 8], P(None, ('groups', 'expert')), parts along dimension 1, may hold values from 0.1 to 1
Outputs:
- mixed: bfloat16 [2, 2048, 2048], P(None, ('groups', 'expert')), parts along dimension 1
The draws below stay inside these ranges and needn't reach their ends.
There are 2 independent parts, one for each index of `groups`. The reference program is written for one: setup_inputs(seed, part) draws one part's arguments, and reference() takes and returns one part's arrays. A program takes and returns all parts, laid end to end along the dimension named above; an argument that names none is the same for every part. Nothing has to cross between parts.
Inputs may be any that keep to these rules, and one draw needn't show every extreme that they name: `hot_pick`: in each aligned block of 64 tokens of one micro-batch, each hot expert is picked by exactly 32 tokens. `cold_routes`: A token names 8 - 1 different cold experts; in each aligned block of 64 tokens of one micro-batch no cold expert is named more than 43 times.
All inputs are finite; a program needn't handle non-finite values.
Results may differ from the reference program's by a relative error of at most 0.0058.
Values may be sent and summed in bfloat16 or wider, within the bound.
No kernel may reach another device: no remote copies, remote signals or barrier semaphores. Data moves between devices by JAX's collectives and lax.ppermute only.
A program may use at most 128 MiB of HBM per device.

```python
import math
import jax
import jax.numpy as jnp
import numpy as np
from jax import lax

D = 2048
FF = 768
TOP = 8
HOT = 2
MB = 2
TOK_DEV = 64
COLD = 16
TOKENS = 1024
CAP = 43
N_EXPERT = 16


def draw_hot_pick(key, part):
    blocks = MB * TOKENS // TOK_DEV
    keys = jax.random.split(key, blocks)

    def one_block(block_key):
        return jax.random.permutation(block_key, TOK_DEV)
    orders = jax.vmap(one_block)(keys)
    return (orders % HOT).astype(jnp.int32).reshape(MB, TOKENS)


def block_scale(own_key, extent, cuts, smallest, top_value):
    def one(position, shards_of):
        heights = jax.random.uniform(jax.random.fold_in(jax.random.fold_in(own_key, 6), position), (shards_of,), jnp.float32, smallest / len(cuts), top_value / len(cuts))
        return jnp.repeat(jnp.exp(heights), extent[position] // shards_of).reshape((-1,) + (1,) * (len(extent) - position - 1))

    level = one(*cuts[0])
    for cut in cuts[1:]:
        level = level * one(*cut)
    return level


def deal_out(own_key, own, number, rows, amount, top, most, slope):
    sequence = jax.random.permutation(own_key, amount)
    packed, common = shares(amount, rows * top, most, slope, True), shares(amount, rows * top, most, slope, False)
    places = jnp.arange(amount)

    def named(sizes, offset_by):
        used = int((sizes > 0).sum())
        fixed = max(1, used // 4)
        moved = fixed + (places - fixed + offset_by * (used - fixed)) % max(1, amount - fixed)
        return jnp.zeros((amount,), jnp.int32).at[sequence[jnp.where(places < fixed, places, moved)]].set(jnp.asarray(sizes, jnp.int32))

    sizes = jnp.where(number % 4 == 0, named(packed, number // 4), named(common, number - number // 4 - 1))
    mixed = jax.random.permutation(jax.random.fold_in(own, 3), amount)
    source_of, taker = mixed[0:amount // 2 * 2:2], mixed[1:amount // 2 * 2:2]
    room = jnp.minimum(sizes[source_of] - 1, most - sizes[taker]) // 2
    room = jnp.where((source_of == sequence[0]) | (taker == sequence[0]) | (sizes[taker] == 0), 0, jnp.maximum(room, 0))
    moved = jax.random.randint(jax.random.fold_in(own, 4), (amount // 2,), 0, 1 << 20) % (room + 1)
    sizes = sizes.at[source_of].add(-moved).at[taker].add(moved)
    labels = jnp.searchsorted(jnp.cumsum(sizes), jnp.arange(rows * top), side="right").astype(jnp.int32)
    table = labels.reshape(top, rows).T
    table = table[jax.random.permutation(jax.random.fold_in(own, 1), rows)]
    offset_by = jax.random.randint(jax.random.fold_in(own, 2), (rows, 1), 0, top)
    return jnp.take_along_axis(table, (jnp.arange(top)[None, :] + offset_by) % top, axis=1)


def shares(number_of, total, reach, slope, full):
    loads = [(1 << 20) // math.isqrt(rank ** slope) + 1 for rank in range(1, number_of + 1)]
    largest = reach if full else min(reach, max(-(-total // number_of), total * loads[0] // sum(loads)))
    least = 1 if total - largest >= number_of - 1 else 0
    holding, spare = [largest] + [least] * (number_of - 1), total - largest - least * (number_of - 1)
    while spare > 0:
        candidates = [i for i in range(1, number_of) if holding[i] < largest] or [i for i in range(1, number_of) if holding[i] < reach]
        mass, budget = sum([loads[i] for i in candidates]), spare
        for i in candidates:
            more = min(reach - holding[i], max(1, budget * loads[i] // mass), spare)
            holding[i] = holding[i] + more
            spare = spare - more
    return np.array(holding)


def noise(stream_key, shape, width, most, cuts=(), kind=jnp.bfloat16):
    loudness = block_scale(stream_key, shape, cuts, -0.22, 0.18) if cuts else 1.0
    array = jax.random.normal(stream_key, shape, jnp.float32) * width * loudness
    return jnp.minimum(jnp.maximum(array, -most), most).astype(kind)


def setup_inputs(seed: int = 0, part: int = 0) -> dict:
    seeds = jax.random.split(jax.random.key(seed), 11)
    part_splits = jax.random.split(jax.random.fold_in(seeds[10], part), 11)
    tokens = noise(part_splits[0], (MB, TOKENS, D), 1.0, 6.0, ((1, 16),))
    w_gate = noise(seeds[1], (COLD, D, FF), D ** -0.5, 0.125, ((0, 16),))
    w_up = noise(seeds[2], (COLD, D, FF), D ** -0.5, 0.125, ((0, 16),))
    w_down = noise(seeds[3], (COLD, FF, D), FF ** -0.5, 0.21875, ((0, 16),))
    hot_gate = noise(seeds[4], (HOT, D, FF), D ** -0.5, 0.125, ((2, 16),))
    hot_up = noise(seeds[5], (HOT, D, FF), D ** -0.5, 0.125, ((2, 16),))
    hot_down = noise(seeds[6], (HOT, D, FF), FF ** -0.5, 0.21875, ((2, 16),))
    cold_routes_keys = jax.random.split(jax.random.fold_in(part_splits[7], 1), MB * TOKENS // TOK_DEV)
    cold_routes_turns = jax.random.permutation(jax.random.fold_in(part_splits[7], 3), MB * TOKENS // TOK_DEV)
    cold_routes = jax.vmap(lambda own, number: deal_out(jax.random.fold_in(part_splits[7], 2), own, number, TOK_DEV, COLD, TOP - 1, CAP, 2))(cold_routes_keys, cold_routes_turns).reshape((MB, TOKENS, TOP - 1))
    hot_pick = draw_hot_pick(jax.random.fold_in(jax.random.fold_in(seeds[10], part), 71), part)
    gates = jnp.clip(jnp.exp(math.log(1.0) - 2.3025851 * jax.random.uniform(part_splits[9], (MB, TOKENS, TOP), jnp.float32) ** block_scale(part_splits[9], (MB, TOKENS, TOP), ((1, 16),), -0.2, 0.2)), 0.1, 1.0)
    return {"tokens": tokens, "w_gate": w_gate, "w_up": w_up, "w_down": w_down, "hot_gate": hot_gate, "hot_up": hot_up, "hot_down": hot_down, "cold_routes": cold_routes, "hot_pick": hot_pick, "gates": gates}


def expert_rows(rows_in, gate_one, up_one, down_one):
    gate = jnp.dot(rows_in, gate_one, preferred_element_type=jnp.float32)
    upward = jnp.dot(rows_in, up_one, preferred_element_type=jnp.float32)
    hidden = (jax.nn.silu(gate) * upward).astype(jnp.bfloat16)
    return jnp.dot(hidden, down_one, preferred_element_type=jnp.float32).astype(jnp.bfloat16)


def reference(tokens, w_gate, w_up, w_down, hot_gate, hot_up, hot_down, cold_routes, hot_pick, gates):
    all_rows = MB * TOKENS
    picks = TOP - 1
    flat = tokens.reshape(all_rows, D)
    expert = cold_routes.reshape(all_rows * picks)
    owner = jnp.repeat(jnp.arange(all_rows, dtype=jnp.int32), picks)
    weight = gates[:, :, 1:].reshape(all_rows * picks)
    bound = MB * N_EXPERT * CAP

    def visit(carry, number):
        chosen = expert == number
        found = jnp.nonzero(chosen, size=bound, fill_value=0)[0].astype(jnp.int32)
        live = jnp.arange(bound, dtype=jnp.int32) < jnp.sum(chosen.astype(jnp.int32))
        rows_at = owner[found]
        result = expert_rows(flat[rows_at], w_gate[number], w_up[number], w_down[number])
        scaled = jnp.where(live, weight[found], jnp.zeros_like(weight[found]))[:, None] * result.astype(jnp.float32)
        return carry.at[rows_at].add(scaled), None

    total = jnp.zeros((all_rows, D), jnp.float32)
    total, unused = lax.scan(visit, total, jnp.arange(COLD, dtype=jnp.int32))
    pick_flat = hot_pick.reshape(all_rows)
    share = all_rows // HOT
    hot_gate_row = gates[:, :, 0].reshape(all_rows)
    for number in range(HOT):
        found = jnp.nonzero(pick_flat == number, size=share, fill_value=0)[0].astype(jnp.int32)
        result = expert_rows(flat[found], hot_gate[number], hot_up[number], jnp.transpose(hot_down[number]))
        total = total.at[found].add(hot_gate_row[found][:, None] * result.astype(jnp.float32))
    return total.astype(jnp.bfloat16).reshape(MB, TOKENS, D)
```

```python
import jax
import jax.numpy as jnp
from jax import lax
from jax.sharding import PartitionSpec as P


def ring_tables(devices):
    chips = devices // 2
    ring = list(range(0, chips, 2)) + list(range(chips - 1, 0, -2))
    around = []
    for place in range(chips):
        following, preceding = ring[(place + 1) % chips], ring[place - 1]
        around.append((2 * ring[place], 2 * following))
        around.append((2 * ring[place] + 1, 2 * preceding + 1))
    across = [(device, device ^ 1) for device in range(devices)]
    return ring, around, across


def shards(tokens, w_gate, w_up, w_down, hot_gate, hot_up, hot_down, cold_routes, hot_pick, gates):
    devices = lax.axis_size("expert")
    micros, held, width = tokens.shape
    hots, hot_hidden = hot_gate.shape[0], hot_gate.shape[2]
    chips = devices // 2
    half = chips // 2
    ring, around, across = ring_tables(devices)
    me = lax.axis_index("expert")
    core = me % 2

    named = cold_routes[..., None] == jnp.arange(devices, dtype=jnp.int32)
    spread = jnp.sum(jnp.where(named, gates[..., 1:, None], 0.0), axis=2)
    facts = jnp.concatenate(
        [spread, gates[..., :1], hot_pick[..., None].astype(jnp.float32)], axis=-1
    )
    facts = lax.all_gather(facts, "expert", axis=0)
    place_of = [0] * chips
    for place, chip in enumerate(ring):
        place_of[chip] = place
    place = jnp.array(place_of, jnp.int32)[me // 2]
    turn = 1 - 2 * core
    steps = (place - turn * jnp.arange(chips, dtype=jnp.int32)) % chips
    order = 2 * jnp.array(ring, jnp.int32)[steps][:, None] + (core ^ jnp.arange(2, dtype=jnp.int32))
    facts = facts[order]
    own_column = jnp.arange(devices, dtype=jnp.int32) == me
    cold_weight = jnp.sum(jnp.where(own_column, facts[..., :devices], 0.0), axis=-1)
    hot_weight, hot_number = facts[..., devices], facts[..., devices + 1]

    hot_in = jnp.concatenate([hot_gate[h] for h in range(hots)] + [hot_up[h] for h in range(hots)], axis=1)
    hot_out = jnp.concatenate([hot_down[h] for h in range(hots)], axis=1)
    hot_of = jnp.arange(hots * hot_hidden, dtype=jnp.int32) // hot_hidden
    hot_of = hot_of.astype(jnp.float32)

    def contribution(rows, weight, hot_w, hot_n):
        gate = jnp.dot(rows, w_gate[0], preferred_element_type=jnp.float32)
        up = jnp.dot(rows, w_up[0], preferred_element_type=jnp.float32)
        hidden = (jax.nn.silu(gate) * up).astype(jnp.bfloat16)
        cold = jnp.dot(hidden, w_down[0], preferred_element_type=jnp.float32)
        both = jnp.dot(rows, hot_in, preferred_element_type=jnp.float32)
        split = hots * hot_hidden
        hot_h = jax.nn.silu(both[:, :split]) * both[:, split:]
        hot_h = jnp.where(hot_n[:, None] == hot_of[None, :], hot_h, 0.0).astype(jnp.bfloat16)
        hot = lax.dot_general(
            hot_h, hot_out, (((1,), (1,)), ((), ())), preferred_element_type=jnp.float32
        )
        return (weight[:, None] * cold + hot_w[:, None] * hot).astype(jnp.bfloat16)

    def of_rows(table, micro, step, flip):
        first, second = table[step % chips, 0, micro], table[step % chips, 1, micro]
        return [second, first] if flip else [first, second]

    def joined(table, micro, step):
        if step == 0:
            parts = of_rows(table, micro, 0, False)
        elif step == half:
            parts = of_rows(table, micro, half, False)
        else:
            parts = of_rows(table, micro, step, False) + of_rows(table, micro, chips - step, True)
        return jnp.concatenate(parts)

    def swap(x):
        return lax.ppermute(x, "expert", across)

    def onward(x):
        return lax.ppermute(x, "expert", around)

    def work(rows, micro, step):
        return contribution(
            rows,
            joined(cold_weight, micro, step),
            joined(hot_weight, micro, step),
            joined(hot_number, micro, step),
        )

    made = [[None] * (half + 1) for _ in range(micros)]
    mine = [None] * micros
    for micro in range(micros):
        rows = jnp.concatenate([tokens[micro], swap(tokens[micro])])
        mine[micro] = rows
        made[micro][0] = rows
    for step in range(1, half + 1):
        for micro in range(micros):
            sent = mine[micro] if step < half else mine[micro][:held]
            mine[micro] = onward(sent)
            made[micro][step] = jnp.concatenate([mine[micro], swap(mine[micro])])
    for micro in range(micros):
        for step in range(half + 1):
            made[micro][step] = work(made[micro][step], micro, step)

    outs = [None] * micros
    coming = [None] * micros
    for step in range(half, 0, -1):
        for micro in range(micros):
            own = made[micro][step]
            middle = own.shape[0] // 2
            other = swap(own[:middle])
            total = own[middle:].astype(jnp.float32) + other.astype(jnp.float32)
            if coming[micro] is not None:
                extra = coming[micro].astype(jnp.float32)
                if extra.shape[0] < total.shape[0]:
                    extra = jnp.concatenate([extra, jnp.zeros_like(extra)])
                total = total + extra
            coming[micro] = onward(total.astype(jnp.bfloat16))
    for micro in range(micros):
        own = made[micro][0].astype(jnp.float32)
        extra = coming[micro].astype(jnp.float32)
        away = swap((own[held:] + extra[:held]).astype(jnp.bfloat16))
        outs[micro] = (own[:held] + extra[held:] + away.astype(jnp.float32)).astype(jnp.bfloat16)
    return jnp.stack(outs)


def solution(mesh):
    in_specs = (
        P(None, ("groups", "expert"), None),
        P("expert", None, None),
        P("expert", None, None),
        P("expert", None, None),
        P(None, None, "expert"),
        P(None, None, "expert"),
        P(None, None, "expert"),
        P(None, ("groups", "expert"), None),
        P(None, ("groups", "expert")),
        P(None, ("groups", "expert"), None),
    )
    out_specs = P(None, ("groups", "expert"), None)
    return jax.shard_map(shards, mesh=mesh, in_specs=in_specs, out_specs=out_specs, check_vma=False)
```

```python
import functools

import jax
import jax.numpy as jnp
from jax import lax
from jax.experimental import pallas as pl
from jax.experimental.pallas import tpu as pltpu
from jax.sharding import PartitionSpec as P

LANES = 128
PIECE = 32
SLOT = 8
HOT_GATE = 2 * PIECE
HOT_PICK = HOT_GATE + 3


def ring_tables(devices):
    chips = devices // 2
    ring = list(range(0, chips, 2)) + list(range(chips - 1, 0, -2))
    around = []
    for place in range(chips):
        following, preceding = ring[(place + 1) % chips], ring[place - 1]
        around.append((2 * ring[place], 2 * following))
        around.append((2 * ring[place] + 1, 2 * preceding + 1))
    across = [(device, device ^ 1) for device in range(devices)]
    return around, across


def tile_of(size, most):
    tile = most
    while size % tile:
        tile //= 2
    return tile


def silu(value):
    return value / (1.0 + jnp.exp(-value))


def work_body(me_ref, mine, shared, gate, up, down, hot_in, hot_out, y_mine, y_shared, rows, hidden, hot_hidden, *, hots):
    count, width = y_mine.shape
    units = gate.shape[1]
    rows[:count] = mine[:, :width]
    rows[count:] = shared[:, :width]
    facts = jnp.concatenate([mine[:, width:], shared[:, width:]], axis=0).astype(jnp.float32)
    lane = lax.broadcasted_iota(jnp.int32, facts.shape, 1)
    named = (facts == me_ref[0].astype(jnp.float32)) & (lane < 3 * SLOT)
    pieces = pltpu.roll(facts, LANES - PIECE, 1)
    cold_weight = jnp.sum(jnp.where(named, pieces, 0.0), axis=1, keepdims=True)
    is_hot = (lane >= HOT_GATE) & (lane < HOT_PICK)
    hot_weight = jnp.sum(jnp.where(is_hot, facts, 0.0), axis=1, keepdims=True)
    hot_pick = jnp.sum(jnp.where(lane == HOT_PICK, facts, 0.0), axis=1, keepdims=True)

    split = hot_in.shape[1] // 2
    both = jnp.dot(rows[...], hot_in[...], preferred_element_type=jnp.float32)
    value = silu(both[:, :split]) * both[:, split:]
    owner = lax.broadcasted_iota(jnp.int32, value.shape, 1) // (split // hots)
    hot_hidden[...] = jnp.where(owner.astype(jnp.float32) == hot_pick, value, 0.0).astype(jnp.bfloat16)

    tile = tile_of(units, 256)
    for start in range(0, units, tile):
        cut = slice(start, start + tile)
        a = jnp.dot(rows[...], gate[:, cut], preferred_element_type=jnp.float32)
        b = jnp.dot(rows[...], up[:, cut], preferred_element_type=jnp.float32)
        hidden[:, cut] = (silu(a) * b).astype(jnp.bfloat16)
    tile = tile_of(width, 512)
    for start in range(0, width, tile):
        cut = slice(start, start + tile)
        y = cold_weight * jnp.dot(hidden[...], down[:, cut], preferred_element_type=jnp.float32)
        y = y + hot_weight * jnp.dot(hot_hidden[...], hot_out[:, cut], preferred_element_type=jnp.float32)
        y_mine[:, cut] = y[:count].astype(y_mine.dtype)
        y_shared[:, cut] = y[count:].astype(y_shared.dtype)


def work(me, mine, shared, weights, hots):
    count = mine.shape[0]
    width, units = weights[0].shape
    hot_units = weights[4].shape[0]
    whole = pl.BlockSpec(memory_space=pltpu.VMEM)
    return pl.pallas_call(
        functools.partial(work_body, hots=hots),
        in_specs=[pl.BlockSpec(memory_space=pltpu.SMEM)] + [whole] * 7,
        out_specs=[whole] * 2,
        out_shape=[jax.ShapeDtypeStruct((count, width), jnp.bfloat16)] * 2,
        scratch_shapes=[
            pltpu.VMEM((2 * count, width), jnp.bfloat16),
            pltpu.VMEM((2 * count, units), jnp.bfloat16),
            pltpu.VMEM((2 * count, hot_units), jnp.bfloat16),
        ],
        compiler_params=pltpu.CompilerParams(vmem_limit_bytes=40 << 20),
        cost_estimate=pl.CostEstimate(
            flops=2 * 2 * count * width * 3 * (units + hot_units),
            bytes_accessed=2 * 4 * count * width,
            transcendentals=2 * count * units,
        ),
    )(me, mine, shared, *weights)


def facts_of(cold_routes, hot_pick, gates):
    high = lax.reduce_precision(gates, 8, 7)
    middle = lax.reduce_precision(gates - high, 8, 7)
    low = gates - high - middle
    pieces = [high, middle, low]
    lead = gates.shape[:-1]
    picks = cold_routes.astype(jnp.float32)
    gap = jnp.full(lead + (SLOT - picks.shape[-1],), -1.0, jnp.float32)
    hollow = jnp.zeros(lead + (SLOT - picks.shape[-1],), jnp.float32)
    columns = [picks, gap] * 3 + [jnp.zeros(lead + (PIECE - 3 * SLOT,), jnp.float32)]
    for piece in pieces:
        columns += [piece[..., 1:], hollow]
    columns += [jnp.zeros(lead + (PIECE - 3 * SLOT,), jnp.float32)]
    columns += [piece[..., :1] for piece in pieces] + [hot_pick[..., None].astype(jnp.float32)]
    columns += [jnp.zeros(lead + (LANES - HOT_PICK - 1,), jnp.float32)]
    return jnp.concatenate(columns, axis=-1).astype(jnp.bfloat16)


def shards(tokens, w_gate, w_up, w_down, hot_gate, hot_up, hot_down, cold_routes, hot_pick, gates):
    devices = lax.axis_size("expert")
    micros, held, width = tokens.shape
    hots = hot_gate.shape[0]
    chips = devices // 2
    around, across = ring_tables(devices)
    me = lax.axis_index("expert").astype(jnp.int32).reshape(1)

    def swap(x):
        return lax.ppermute(x, "expert", across)

    def onward(x):
        return lax.ppermute(x, "expert", around)

    rows = jnp.concatenate([tokens, facts_of(cold_routes, hot_pick, gates)], axis=-1)
    rows = rows.reshape(micros * held, rows.shape[-1])
    hot_in = jnp.concatenate([w[h] for w in (hot_gate, hot_up) for h in range(hots)], axis=1)
    hot_out = jnp.concatenate([hot_down[h].T for h in range(hots)], axis=0)
    weights = (w_gate[0], w_up[0], w_down[0], hot_in, hot_out)

    own = work(me, rows, swap(rows), weights, hots)
    coming = None
    mine = rows
    for step in range(1, chips):
        mine = onward(mine)
        kept, given = work(me, mine, swap(mine), weights, hots)
        total = kept.astype(jnp.float32) + swap(given).astype(jnp.float32)
        if coming is not None:
            total = total + coming.astype(jnp.float32)
        coming = onward(total.astype(jnp.bfloat16))
    total = own[0].astype(jnp.float32) + swap(own[1]).astype(jnp.float32) + coming.astype(jnp.float32)
    return total.astype(jnp.bfloat16).reshape(micros, held, width)


def solution(mesh):
    in_specs = (
        P(None, ("groups", "expert"), None),
        P("expert", None, None),
        P("expert", None, None),
        P("expert", None, None),
        P(None, None, "expert"),
        P(None, None, "expert"),
        P(None, None, "expert"),
        P(None, ("groups", "expert"), None),
        P(None, ("groups", "expert")),
        P(None, ("groups", "expert"), None),
    )
    out_specs = P(None, ("groups", "expert"), None)
    return jax.shard_map(shards, mesh=mesh, in_specs=in_specs, out_specs=out_specs, check_vma=False)
```

```python
import functools

import jax
import jax.numpy as jnp
from jax import lax
from jax.experimental import pallas as pl
from jax.experimental.pallas import tpu as pltpu
from jax.sharding import PartitionSpec as P

LANES = 128
PIECE = 32
SLOT = 8
HOT_GATE = 2 * PIECE
HOT_PICK = HOT_GATE + 3
FIRST_PARTS = 1
MERGE_AT = 3
OWN_AT = 1
LAST_PARTS = 1
LAST_STEPS = 2
ORDERED = True


def ring_tables(devices):
    chips = devices // 2
    ring = list(range(0, chips, 2)) + list(range(chips - 1, 0, -2))
    around = []
    for place in range(chips):
        following, preceding = ring[(place + 1) % chips], ring[place - 1]
        around.append((2 * ring[place], 2 * following))
        around.append((2 * ring[place] + 1, 2 * preceding + 1))
    across = [(device, device ^ 1) for device in range(devices)]
    return around, across


def tile_of(size, most):
    tile = most
    while size % tile:
        tile //= 2
    return tile


def silu(value):
    return value / (1.0 + jnp.exp(-value))


def rows_body(tokens, gates, routes, pick, *refs, micros, parts):
    outs, (gates_in, routes_in, pick_in, columns, done) = refs[:parts], refs[parts:]
    held, width = tokens.shape[1:]
    picks = routes.shape[0]
    share = micros // parts
    copies = [
        pltpu.make_async_copy(source, target, done.at[number])
        for number, (source, target) in enumerate(((gates, gates_in), (routes, routes_in), (pick, pick_in)))
    ]
    places = []
    for micro in range(micros):
        places.append((outs[micro // share], pl.ds(micro % share * held, held)))
        out, place = places[-1]
        copies.append(pltpu.make_async_copy(tokens.at[micro], out.at[place, pl.ds(0, width)], done.at[3 + micro]))
    for copy in copies:
        copy.start()
    for copy in copies[:3]:
        copy.wait()
    for micro in range(micros):
        columns[...] = jnp.full(columns.shape, 0.0, jnp.float32)
        rest = gates_in[micro]
        for piece in range(3):
            part = rest.astype(jnp.bfloat16).astype(jnp.float32)
            rest = rest - part
            columns[HOT_GATE + piece : HOT_GATE + piece + 1] = part[:1]
            columns[PIECE + piece * SLOT : PIECE + piece * SLOT + picks] = part[1:]
            columns[piece * SLOT + picks : (piece + 1) * SLOT] = jnp.full((SLOT - picks, held), -1.0, jnp.float32)
            for k in range(picks):
                row = piece * SLOT + k
                columns[row : row + 1] = routes_in[k, micro : micro + 1].astype(jnp.float32)
        columns[HOT_PICK : HOT_PICK + 1] = pick_in[micro : micro + 1].astype(jnp.float32)
        out, place = places[micro]
        out[place, width:] = columns[...].T.astype(jnp.bfloat16)
    for copy in copies[3:]:
        copy.wait()


def in_place(arrays):
    return [pltpu.with_memory_space_constraint(array, pltpu.HBM) for array in arrays]


def build_rows(tokens, cold_routes, hot_pick, gates, parts):
    micros, held, width = tokens.shape
    whole = pl.BlockSpec(memory_space=pltpu.VMEM)
    return pl.pallas_call(
        functools.partial(rows_body, micros=micros, parts=parts),
        in_specs=[pl.BlockSpec(memory_space=pltpu.HBM)] * 4,
        out_specs=[whole] * parts,
        out_shape=[jax.ShapeDtypeStruct((micros // parts * held, width + LANES), jnp.bfloat16)] * parts,
        scratch_shapes=[
            pltpu.VMEM((micros, gates.shape[-1], held), jnp.float32),
            pltpu.VMEM((cold_routes.shape[-1], micros, held), jnp.int32),
            pltpu.VMEM((micros, held), jnp.int32),
            pltpu.VMEM((LANES, held), jnp.float32),
            pltpu.SemaphoreType.DMA((3 + micros,)),
        ],
        compiler_params=pltpu.CompilerParams(vmem_limit_bytes=8 << 20),
        cost_estimate=pl.CostEstimate(flops=0, bytes_accessed=4 * micros * held * width, transcendentals=0),
    )(*in_place([tokens, jnp.swapaxes(gates, 1, 2), jnp.transpose(cold_routes, (2, 0, 1)), hot_pick]))


def load_body(me_ref, *refs, parts, hots, hot_parts):
    blocks, refs = refs[: 2 * parts], refs[2 * parts :]
    far, refs = refs[: 4 + hot_parts], refs[4 + hot_parts :]
    outs, near, scratch, done = refs[:2], refs[2:7], refs[7:10], refs[10]
    copies, offset = [[], [], [], []], 0

    def add(group, source, target):
        number = sum(len(waiting) for waiting in copies)
        copies[group].append(pltpu.make_async_copy(source, target, done.at[number]))

    for part in far[4:]:
        add(0, part, near[3].at[pl.ds(offset, part.shape[0])])
        offset += part.shape[0]
    units = near[0].shape[1]
    tile = tile_of(units, 256)
    for start in range(0, units, tile):
        for source, target in zip(far[:2], near[:2]):
            add(1, source.at[:, pl.ds(start, tile)], target.at[:, pl.ds(start, tile)])
    add(2, far[2], near[2])
    add(3, far[3], near[4])
    for group in copies:
        for copy in group:
            copy.start()

    def ready(group, number):
        if group == 1:
            copies[1][2 * number].wait()
            copies[1][2 * number + 1].wait()
            return
        for copy in copies[group]:
            copy.wait()

    work_body(me_ref, *blocks, *near, *outs, *scratch, parts=parts, hots=hots, ready=ready)


def work_body(me_ref, *refs, parts, hots, ready=lambda group, number: None):
    blocks, refs = refs[: 2 * parts], refs[2 * parts :]
    (gate, up, down, hot_in, hot_out), (y_mine, y_shared), (rows, hidden, hot_hidden) = refs[:5], refs[5:7], refs[7:]
    count, width = y_mine.shape
    units = gate.shape[1]
    start = 0
    for block in blocks:
        rows[start : start + block.shape[0]] = block[:, :width]
        start += block.shape[0]
    facts = jnp.concatenate([block[:, width:] for block in blocks], axis=0).astype(jnp.float32)
    lane = lax.broadcasted_iota(jnp.int32, facts.shape, 1)
    named = (facts == me_ref[0].astype(jnp.float32)) & (lane < 3 * SLOT)
    pieces = pltpu.roll(facts, LANES - PIECE, 1)
    cold_weight = jnp.sum(jnp.where(named, pieces, 0.0), axis=1, keepdims=True)
    is_hot = (lane >= HOT_GATE) & (lane < HOT_PICK)
    hot_weight = jnp.sum(jnp.where(is_hot, facts, 0.0), axis=1, keepdims=True)
    hot_pick = jnp.sum(jnp.where(lane == HOT_PICK, facts, 0.0), axis=1, keepdims=True)

    split = hot_in.shape[0] // 2
    ready(0, 0)
    both = lax.dot_general(
        rows[...], hot_in[...], (((1,), (1,)), ((), ())), preferred_element_type=jnp.float32
    )
    value = silu(both[:, :split]) * both[:, split:]
    owner = lax.broadcasted_iota(jnp.int32, value.shape, 1) // (split // hots)
    hot_hidden[...] = jnp.where(owner.astype(jnp.float32) == hot_pick, value, 0.0).astype(jnp.bfloat16)

    tile = tile_of(units, 256)
    for start in range(0, units, tile):
        cut = slice(start, start + tile)
        ready(1, start // tile)
        a = jnp.dot(rows[...], gate[:, cut], preferred_element_type=jnp.float32)
        b = jnp.dot(rows[...], up[:, cut], preferred_element_type=jnp.float32)
        hidden[:, cut] = (silu(a) * b).astype(jnp.bfloat16)
    ready(2, 0)
    ready(3, 0)
    tile = tile_of(width, 512)
    for start in range(0, width, tile):
        cut = slice(start, start + tile)
        y = cold_weight * jnp.dot(hidden[...], down[:, cut], preferred_element_type=jnp.float32)
        y = y + hot_weight * jnp.dot(hot_hidden[...], hot_out[:, cut], preferred_element_type=jnp.float32)
        y_mine[:, cut] = y[:count].astype(y_mine.dtype)
        y_shared[:, cut] = y[count:].astype(y_shared.dtype)


def work(me, mine, shared, weights, hots, bring=False):
    count, parts = sum(part.shape[0] for part in mine), len(mine)
    width, units = weights[0].shape
    whole, far = pl.BlockSpec(memory_space=pltpu.VMEM), pl.BlockSpec(memory_space=pltpu.HBM)
    out_shape = [jax.ShapeDtypeStruct((count, width), jnp.bfloat16)] * 2
    hot_units = weights[3 if bring else 4].shape[0]
    scratch = [
        pltpu.VMEM((2 * count, width), jnp.bfloat16),
        pltpu.VMEM((2 * count, units), jnp.bfloat16),
        pltpu.VMEM((2 * count, hot_units), jnp.bfloat16),
    ]
    body = functools.partial(work_body, parts=parts, hots=hots)
    if bring:
        body = functools.partial(load_body, parts=parts, hots=hots, hot_parts=len(weights) - 4)
        shapes = [w.shape for w in weights[:3]] + [(2 * hot_units, width), (hot_units, width)]
        out_shape += [jax.ShapeDtypeStruct(shape, jnp.bfloat16) for shape in shapes]
        scratch += [pltpu.SemaphoreType.DMA((len(weights) + 2 * (units // tile_of(units, 256)) - 2,))]
    return pl.pallas_call(
        body,
        in_specs=[pl.BlockSpec(memory_space=pltpu.SMEM)] + [whole] * (2 * parts) + [far if bring else whole] * len(weights),
        out_specs=[whole] * len(out_shape),
        out_shape=out_shape,
        scratch_shapes=scratch,
        compiler_params=pltpu.CompilerParams(vmem_limit_bytes=24 << 20),
        cost_estimate=pl.CostEstimate(
            flops=2 * 2 * count * width * 3 * (units + hot_units),
            bytes_accessed=2 * 4 * count * width,
            transcendentals=2 * count * units,
        ),
    )(me, *mine, *shared, *(in_place(weights) if bring else weights))


def shards(tokens, w_gate, w_up, w_down, hot_gate, hot_up, hot_down, cold_routes, hot_pick, gates):
    devices = lax.axis_size("expert")
    micros, held, width = tokens.shape
    hots, _, hot_units = hot_gate.shape
    chips = devices // 2
    around, across = ring_tables(devices)
    me = lax.axis_index("expert").astype(jnp.int32).reshape(1)

    def swap(parts):
        return [lax.ppermute(part, "expert", across) for part in parts]

    def onward(parts):
        return [lax.ppermute(part, "expert", around) for part in parts]

    rows = build_rows(tokens, cold_routes, hot_pick, gates, FIRST_PARTS)
    flat = [jnp.swapaxes(w, 1, 2).reshape(hots * hot_units, width) for w in (hot_gate, hot_up, hot_down)]
    hot_in = flat[:2] if hots * hot_units % 16 == 0 else [jnp.concatenate(flat[:2])]
    weights = (w_gate[0], w_up[0], w_down[0], flat[2], *hot_in)

    own = work(me, rows, swap(rows), weights, hots, bring=True)
    own, weights = own[:2], own[2:]
    coming, total = None, None
    mine = rows
    for step in range(1, chips):
        if step == MERGE_AT and len(mine) > 1:
            mine = [jnp.concatenate(mine)]
        mine = onward(mine)
        if step == OWN_AT:
            mine, own = lax.optimization_barrier((mine, own))
        if total is not None:
            me, total = lax.optimization_barrier((me, total))
            coming = onward(total)
        kept, given = work(me, mine, swap(mine), weights, hots)
        (taken,) = swap([given])
        parts = LAST_PARTS if step >= chips - LAST_STEPS else 1
        total = add_parts(kept, taken, coming, parts)
    coming = onward(total)
    (taken,) = swap([own[1]])
    outs = add_parts(own[0], taken, coming, len(coming))
    return jnp.concatenate(outs).reshape(micros, held, width)


def add_parts(kept, taken, coming, parts):
    size = kept.shape[0] // parts
    sums = []
    for part in range(parts):
        cut = slice(part * size, (part + 1) * size)
        total = kept[cut].astype(jnp.float32) + taken[cut].astype(jnp.float32)
        if coming is not None:
            before = coming[part] if len(coming) == parts else coming[0][cut]
            if ORDERED and sums:
                before, sums[-1] = lax.optimization_barrier((before, sums[-1]))
            total = total + before.astype(jnp.float32)
        sums.append(total.astype(jnp.bfloat16))
    return sums


def solution(mesh):
    in_specs = (
        P(None, ("groups", "expert"), None),
        P("expert", None, None),
        P("expert", None, None),
        P("expert", None, None),
        P(None, None, "expert"),
        P(None, None, "expert"),
        P(None, None, "expert"),
        P(None, ("groups", "expert"), None),
        P(None, ("groups", "expert")),
        P(None, ("groups", "expert"), None),
    )
    out_specs = P(None, ("groups", "expert"), None)
    return jax.shard_map(shards, mesh=mesh, in_specs=in_specs, out_specs=out_specs, check_vma=False)
```

```python
import functools

import jax
import jax.numpy as jnp
from jax import lax
from jax.experimental import pallas as pl
from jax.experimental.pallas import tpu as pltpu
from jax.sharding import PartitionSpec as P

LANES = 128


def ring_tables(devices):
    chips = devices // 2
    ring = list(range(0, chips, 2)) + list(range(chips - 1, 0, -2))
    around = []
    for place in range(chips):
        following, preceding = ring[(place + 1) % chips], ring[place - 1]
        around.append((2 * ring[place], 2 * following))
        around.append((2 * ring[place] + 1, 2 * preceding + 1))
    across = [(device, device ^ 1) for device in range(devices)]
    return around, across


def tile_of(size, most):
    tile = most
    while size % tile:
        tile //= 2
    return tile


def silu(value):
    return value / (1.0 + jnp.exp(-value))


def rows_body(tokens, gates, routes, pick, out, tokens_in, gates_in, routes_in, pick_in, columns, done, *, micros):
    held, width = tokens.shape[1:]
    count, slots = micros * held, gates.shape[1]
    group = 4 * slots
    depth = count * group // LANES
    pairs = [(gates, gates_in), (routes, routes_in), (pick, pick_in)]
    pairs += [(tokens.at[micro], tokens_in.at[pl.ds(micro * held, held)]) for micro in range(micros)]
    copies = [pltpu.make_async_copy(*pair, done.at[number]) for number, pair in enumerate(pairs)]
    for copy in copies:
        copy.start()
    for copy in copies[:3]:
        copy.wait()
    for micro in range(micros):
        rest = gates_in[micro]
        pieces = []
        for _ in range(3):
            pieces.append(rest.astype(jnp.bfloat16).astype(jnp.float32))
            rest = rest - pieces[-1]
        for part in range(held // depth):
            start = (micro * (held // depth) + part) * group
            cut = slice(part * depth, (part + 1) * depth)
            for k in range(slots - 1):
                columns[start + k : start + k + 1] = routes_in[k, micro : micro + 1, cut].astype(jnp.float32)
            columns[start + slots - 1 : start + slots] = pick_in[micro : micro + 1, cut].astype(jnp.float32)
            for number, piece in enumerate(pieces):
                columns[start + (number + 1) * slots : start + (number + 2) * slots] = piece[:, cut]
    out[width // LANES * count :] = columns[...].T.astype(jnp.bfloat16)
    for copy in copies[3:]:
        copy.wait()
    for block in range(width // LANES):
        out[block * count : (block + 1) * count] = tokens_in[:, block * LANES : (block + 1) * LANES]


def in_place(arrays):
    return [pltpu.with_memory_space_constraint(array, pltpu.HBM) for array in arrays]


def build_rows(tokens, cold_routes, hot_pick, gates):
    micros, held, width = tokens.shape
    slots, count = gates.shape[-1], micros * held
    depth = count * 4 * slots // LANES
    return pl.pallas_call(
        functools.partial(rows_body, micros=micros),
        in_specs=[pl.BlockSpec(memory_space=pltpu.HBM)] * 4,
        out_specs=pl.BlockSpec(memory_space=pltpu.VMEM),
        out_shape=jax.ShapeDtypeStruct((width // LANES * count + depth, LANES), jnp.bfloat16),
        scratch_shapes=[
            pltpu.VMEM((count, width), jnp.bfloat16),
            pltpu.VMEM((micros, slots, held), jnp.float32),
            pltpu.VMEM((slots - 1, micros, held), jnp.int32),
            pltpu.VMEM((micros, held), jnp.int32),
            pltpu.VMEM((LANES, depth), jnp.float32),
            pltpu.SemaphoreType.DMA((3 + micros,)),
        ],
        compiler_params=pltpu.CompilerParams(vmem_limit_bytes=8 << 20),
        cost_estimate=pl.CostEstimate(flops=0, bytes_accessed=4 * micros * held * width, transcendentals=0),
    )(*in_place([tokens, jnp.swapaxes(gates, 1, 2), jnp.transpose(cold_routes, (2, 0, 1)), hot_pick]))


def load_body(me_ref, *refs, slots, hots, hot_parts):
    blocks, refs = refs[:2], refs[2:]
    far, refs = refs[: 4 + hot_parts], refs[4 + hot_parts :]
    outs, near, scratch, done = refs[:2], refs[2:7], refs[7:10], refs[10]
    copies, offset = [[], [], [], []], 0

    def add(group, source, target):
        number = sum(len(waiting) for waiting in copies)
        copies[group].append(pltpu.make_async_copy(source, target, done.at[number]))

    for part in far[4:]:
        add(0, part, near[3].at[pl.ds(offset, part.shape[0])])
        offset += part.shape[0]
    units = near[0].shape[1]
    tile = tile_of(units, 256)
    for start in range(0, units, tile):
        for source, target in zip(far[:2], near[:2]):
            add(1, source.at[:, pl.ds(start, tile)], target.at[:, pl.ds(start, tile)])
    add(2, far[2], near[2])
    add(3, far[3], near[4])
    for group in copies:
        for copy in group:
            copy.start()

    def ready(group, number):
        if group == 1:
            copies[1][2 * number].wait()
            copies[1][2 * number + 1].wait()
            return
        for copy in copies[group]:
            copy.wait()

    work_body(me_ref, *blocks, *near, *outs, *scratch, slots=slots, hots=hots, ready=ready)


def work_body(me_ref, *refs, slots, hots, ready=lambda group, number: None):
    blocks, refs = refs[:2], refs[2:]
    (gate, up, down, hot_in, hot_out), (y_mine, y_shared), (rows, hidden, hot_hidden) = refs[:5], refs[5:7], refs[7:]
    count, width = y_mine.shape
    units = gate.shape[1]
    group = 4 * slots
    facts = []
    for number, block in enumerate(blocks):
        for column in range(width // LANES):
            place = slice(column * LANES, (column + 1) * LANES)
            rows[number * count : (number + 1) * count, place] = block[column * count : (column + 1) * count]
        packed = block[width // LANES * count :].astype(jnp.float32)
        facts += [pltpu.roll(packed, (LANES - start) % LANES, 1) if start else packed for start in range(0, LANES, group)]
    facts = jnp.concatenate(facts, axis=0)
    lane = lax.broadcasted_iota(jnp.int32, facts.shape, 1)
    named = (facts == me_ref[0].astype(jnp.float32)) & (lane < slots - 1)
    pieces = [pltpu.roll(facts, LANES - slots * number - 1, 1) for number in (1, 2, 3)]
    cold_weight = jnp.sum(jnp.where(named, pieces[0] + pieces[1] + pieces[2], 0.0), axis=1, keepdims=True)
    is_hot = (lane == slots) | (lane == 2 * slots) | (lane == 3 * slots)
    hot_weight = jnp.sum(jnp.where(is_hot, facts, 0.0), axis=1, keepdims=True)
    hot_pick = jnp.sum(jnp.where(lane == slots - 1, facts, 0.0), axis=1, keepdims=True)

    split = hot_in.shape[0] // 2
    ready(0, 0)
    both = lax.dot_general(
        rows[...], hot_in[...], (((1,), (1,)), ((), ())), preferred_element_type=jnp.float32
    )
    value = silu(both[:, :split]) * both[:, split:]
    owner = lax.broadcasted_iota(jnp.int32, value.shape, 1) // (split // hots)
    hot_hidden[...] = jnp.where(owner.astype(jnp.float32) == hot_pick, value, 0.0).astype(jnp.bfloat16)

    tile = tile_of(units, 256)
    for start in range(0, units, tile):
        cut = slice(start, start + tile)
        ready(1, start // tile)
        a = jnp.dot(rows[...], gate[:, cut], preferred_element_type=jnp.float32)
        b = jnp.dot(rows[...], up[:, cut], preferred_element_type=jnp.float32)
        hidden[:, cut] = (silu(a) * b).astype(jnp.bfloat16)
    ready(2, 0)
    ready(3, 0)
    tile = tile_of(width, 512)
    for start in range(0, width, tile):
        cut = slice(start, start + tile)
        y = cold_weight * jnp.dot(hidden[...], down[:, cut], preferred_element_type=jnp.float32)
        y = y + hot_weight * jnp.dot(hot_hidden[...], hot_out[:, cut], preferred_element_type=jnp.float32)
        y_mine[:, cut] = y[:count].astype(y_mine.dtype)
        y_shared[:, cut] = y[count:].astype(y_shared.dtype)


def work(me, mine, shared, weights, slots, hots, bring=False):
    width, units = weights[0].shape
    count = mine.shape[0] * LANES // (width + 4 * slots)
    whole, far = pl.BlockSpec(memory_space=pltpu.VMEM), pl.BlockSpec(memory_space=pltpu.HBM)
    out_shape = [jax.ShapeDtypeStruct((count, width), jnp.bfloat16)] * 2
    hot_units = weights[3 if bring else 4].shape[0]
    scratch = [
        pltpu.VMEM((2 * count, width), jnp.bfloat16),
        pltpu.VMEM((2 * count, units), jnp.bfloat16),
        pltpu.VMEM((2 * count, hot_units), jnp.bfloat16),
    ]
    body = functools.partial(work_body, slots=slots, hots=hots)
    if bring:
        body = functools.partial(load_body, slots=slots, hots=hots, hot_parts=len(weights) - 4)
        shapes = [w.shape for w in weights[:3]] + [(2 * hot_units, width), (hot_units, width)]
        out_shape += [jax.ShapeDtypeStruct(shape, jnp.bfloat16) for shape in shapes]
        scratch += [pltpu.SemaphoreType.DMA((len(weights) + 2 * (units // tile_of(units, 256)) - 2,))]
    return pl.pallas_call(
        body,
        in_specs=[pl.BlockSpec(memory_space=pltpu.SMEM)] + [whole] * 2 + [far if bring else whole] * len(weights),
        out_specs=[whole] * len(out_shape),
        out_shape=out_shape,
        scratch_shapes=scratch,
        compiler_params=pltpu.CompilerParams(vmem_limit_bytes=24 << 20),
        cost_estimate=pl.CostEstimate(
            flops=2 * 2 * count * width * 3 * (units + hot_units),
            bytes_accessed=2 * 4 * count * width,
            transcendentals=2 * count * units,
        ),
    )(me, mine, shared, *(in_place(weights) if bring else weights))


def shards(tokens, w_gate, w_up, w_down, hot_gate, hot_up, hot_down, cold_routes, hot_pick, gates):
    devices = lax.axis_size("expert")
    micros, held, width = tokens.shape
    hots, _, hot_units = hot_gate.shape
    chips = devices // 2
    around, across = ring_tables(devices)
    me = lax.axis_index("expert").astype(jnp.int32).reshape(1)

    def swap(x):
        return lax.ppermute(x, "expert", across)

    def onward(x):
        return lax.ppermute(x, "expert", around)

    rows = build_rows(tokens, cold_routes, hot_pick, gates)
    flat = [jnp.swapaxes(w, 1, 2).reshape(hots * hot_units, width) for w in (hot_gate, hot_up, hot_down)]
    hot_in = flat[:2] if hots * hot_units % 16 == 0 else [jnp.concatenate(flat[:2])]
    weights = (w_gate[0], w_up[0], w_down[0], flat[2], *hot_in)
    slots = gates.shape[-1]

    own = work(me, rows, swap(rows), weights, slots, hots, bring=True)
    own, weights = own[:2], own[2:]
    coming = None
    mine = rows
    for step in range(1, chips):
        mine = onward(mine)
        if step == 1:
            mine, own = lax.optimization_barrier((mine, own))
        kept, given = work(me, mine, swap(mine), weights, slots, hots)
        total = kept.astype(jnp.float32) + swap(given).astype(jnp.float32)
        if coming is not None:
            total = total + coming.astype(jnp.float32)
        coming = onward(total.astype(jnp.bfloat16))
    total = own[0].astype(jnp.float32) + swap(own[1]).astype(jnp.float32) + coming.astype(jnp.float32)
    return total.astype(jnp.bfloat16).reshape(micros, held, width)


def solution(mesh):
    in_specs = (
        P(None, ("groups", "expert"), None),
        P("expert", None, None),
        P("expert", None, None),
        P("expert", None, None),
        P(None, None, "expert"),
        P(None, None, "expert"),
        P(None, None, "expert"),
        P(None, ("groups", "expert"), None),
        P(None, ("groups", "expert")),
        P(None, ("groups", "expert"), None),
    )
    out_specs = P(None, ("groups", "expert"), None)
    return jax.shard_map(shards, mesh=mesh, in_specs=in_specs, out_specs=out_specs, check_vma=False)
```

```python
import functools

import jax
import jax.numpy as jnp
from jax import lax
from jax.experimental import pallas as pl
from jax.experimental.pallas import tpu as pltpu
from jax.sharding import PartitionSpec as P

LANES = 128
SPLIT = 1


def ring_tables(devices):
    chips = devices // 2
    ring = list(range(0, chips, 2)) + list(range(chips - 1, 0, -2))
    around = []
    for place in range(chips):
        following, preceding = ring[(place + 1) % chips], ring[place - 1]
        around.append((2 * ring[place], 2 * following))
        around.append((2 * ring[place] + 1, 2 * preceding + 1))
    across = [(device, device ^ 1) for device in range(devices)]
    return around, across


def tile_of(size, most):
    tile = most
    while size % tile:
        tile //= 2
    return tile


def silu(value):
    return value / (1.0 + jnp.exp(-value))


def rows_body(tokens, gates, routes, pick, out, tokens_in, gates_in, routes_in, pick_in, columns, done, *, micros):
    held, width = tokens.shape[1:]
    count, slots = micros * held, gates.shape[1]
    group = 4 * slots
    depth = count * group // LANES
    pairs = [(gates, gates_in), (routes, routes_in), (pick, pick_in)]
    pairs += [(tokens.at[micro], tokens_in.at[pl.ds(micro * held, held)]) for micro in range(micros)]
    copies = [pltpu.make_async_copy(*pair, done.at[number]) for number, pair in enumerate(pairs)]
    for copy in copies:
        copy.start()
    for copy in copies[:3]:
        copy.wait()
    for micro in range(micros):
        rest = gates_in[micro]
        pieces = []
        for _ in range(3):
            pieces.append(rest.astype(jnp.bfloat16).astype(jnp.float32))
            rest = rest - pieces[-1]
        for part in range(held // depth):
            start = (micro * (held // depth) + part) * group
            cut = slice(part * depth, (part + 1) * depth)
            for k in range(slots - 1):
                columns[start + k : start + k + 1] = routes_in[k, micro : micro + 1, cut].astype(jnp.float32)
            columns[start + slots - 1 : start + slots] = pick_in[micro : micro + 1, cut].astype(jnp.float32)
            for number, piece in enumerate(pieces):
                columns[start + (number + 1) * slots : start + (number + 2) * slots] = piece[:, cut]
    out[width // LANES * count :] = columns[...].T.astype(jnp.bfloat16)
    for copy in copies[3:]:
        copy.wait()
    for block in range(width // LANES):
        out[block * count : (block + 1) * count] = tokens_in[:, block * LANES : (block + 1) * LANES]


def in_place(arrays):
    return [pltpu.with_memory_space_constraint(array, pltpu.HBM) for array in arrays]


def build_rows(tokens, cold_routes, hot_pick, gates):
    micros, held, width = tokens.shape
    slots, count = gates.shape[-1], micros * held
    depth = count * 4 * slots // LANES
    return pl.pallas_call(
        functools.partial(rows_body, micros=micros),
        in_specs=[pl.BlockSpec(memory_space=pltpu.HBM)] * 4,
        out_specs=pl.BlockSpec(memory_space=pltpu.VMEM),
        out_shape=jax.ShapeDtypeStruct((width // LANES * count + depth, LANES), jnp.bfloat16),
        scratch_shapes=[
            pltpu.VMEM((count, width), jnp.bfloat16),
            pltpu.VMEM((micros, slots, held), jnp.float32),
            pltpu.VMEM((slots - 1, micros, held), jnp.int32),
            pltpu.VMEM((micros, held), jnp.int32),
            pltpu.VMEM((LANES, depth), jnp.float32),
            pltpu.SemaphoreType.DMA((3 + micros,)),
        ],
        compiler_params=pltpu.CompilerParams(vmem_limit_bytes=8 << 20),
        cost_estimate=pl.CostEstimate(flops=0, bytes_accessed=4 * micros * held * width, transcendentals=0),
    )(*in_place([tokens, jnp.swapaxes(gates, 1, 2), jnp.transpose(cold_routes, (2, 0, 1)), hot_pick]))


def load_body(me_ref, *refs, slots, hots, hot_parts):
    blocks, refs = refs[:2], refs[2:]
    far, refs = refs[: 4 + hot_parts], refs[4 + hot_parts :]
    outs, near, scratch, done = refs[:2], refs[2:7], refs[7:10], refs[10]
    copies, offset = [[], [], [], []], 0

    def add(group, source, target):
        number = sum(len(waiting) for waiting in copies)
        copies[group].append(pltpu.make_async_copy(source, target, done.at[number]))

    for part in far[4:]:
        add(0, part, near[3].at[pl.ds(offset, part.shape[0])])
        offset += part.shape[0]
    units = near[0].shape[1]
    tile = tile_of(units, 256)
    for start in range(0, units, tile):
        for source, target in zip(far[:2], near[:2]):
            add(1, source.at[:, pl.ds(start, tile)], target.at[:, pl.ds(start, tile)])
    add(2, far[2], near[2])
    add(3, far[3], near[4])
    for group in copies:
        for copy in group:
            copy.start()

    def ready(group, number):
        if group == 1:
            copies[1][2 * number].wait()
            copies[1][2 * number + 1].wait()
            return
        for copy in copies[group]:
            copy.wait()

    work_body(me_ref, *blocks, *near, *outs, *scratch, slots=slots, hots=hots, ready=ready)


def work_body(me_ref, *refs, slots, hots, ready=lambda group, number: None):
    blocks, refs = refs[:2], refs[2:]
    (gate, up, down, hot_in, hot_out), (y_mine, y_shared), (rows, hidden, hot_hidden) = refs[:5], refs[5:7], refs[7:]
    count, width = y_mine.shape
    units = gate.shape[1]
    group = 4 * slots
    facts = []
    for number, block in enumerate(blocks):
        for column in range(width // LANES):
            place = slice(column * LANES, (column + 1) * LANES)
            rows[number * count : (number + 1) * count, place] = block[column * count : (column + 1) * count]
        packed = block[width // LANES * count :].astype(jnp.float32)
        facts += [pltpu.roll(packed, (LANES - start) % LANES, 1) if start else packed for start in range(0, LANES, group)]
    facts = jnp.concatenate(facts, axis=0)
    lane = lax.broadcasted_iota(jnp.int32, facts.shape, 1)
    named = (facts == me_ref[0].astype(jnp.float32)) & (lane < slots - 1)
    pieces = [pltpu.roll(facts, LANES - slots * number - 1, 1) for number in (1, 2, 3)]
    cold_weight = jnp.sum(jnp.where(named, pieces[0] + pieces[1] + pieces[2], 0.0), axis=1, keepdims=True)
    is_hot = (lane == slots) | (lane == 2 * slots) | (lane == 3 * slots)
    hot_weight = jnp.sum(jnp.where(is_hot, facts, 0.0), axis=1, keepdims=True)
    hot_pick = jnp.sum(jnp.where(lane == slots - 1, facts, 0.0), axis=1, keepdims=True)

    split = hot_in.shape[0] // 2
    ready(0, 0)
    both = lax.dot_general(
        rows[...], hot_in[...], (((1,), (1,)), ((), ())), preferred_element_type=jnp.float32
    )
    value = silu(both[:, :split]) * both[:, split:]
    owner = lax.broadcasted_iota(jnp.int32, value.shape, 1) // (split // hots)
    hot_hidden[...] = jnp.where(owner.astype(jnp.float32) == hot_pick, value, 0.0).astype(jnp.bfloat16)

    tile = tile_of(units, 256)
    for start in range(0, units, tile):
        cut = slice(start, start + tile)
        ready(1, start // tile)
        a = jnp.dot(rows[...], gate[:, cut], preferred_element_type=jnp.float32)
        b = jnp.dot(rows[...], up[:, cut], preferred_element_type=jnp.float32)
        hidden[:, cut] = (silu(a) * b).astype(jnp.bfloat16)
    ready(2, 0)
    ready(3, 0)
    tile = tile_of(width, 512)
    for start in range(0, width, tile):
        cut = slice(start, start + tile)
        y = cold_weight * jnp.dot(hidden[...], down[:, cut], preferred_element_type=jnp.float32)
        y = y + hot_weight * jnp.dot(hot_hidden[...], hot_out[:, cut], preferred_element_type=jnp.float32)
        y_mine[:, cut] = y[:count].astype(y_mine.dtype)
        y_shared[:, cut] = y[count:].astype(y_shared.dtype)


def work(me, mine, shared, weights, slots, hots, bring=False):
    width, units = weights[0].shape
    count = mine.shape[0] * LANES // (width + 4 * slots)
    whole, far = pl.BlockSpec(memory_space=pltpu.VMEM), pl.BlockSpec(memory_space=pltpu.HBM)
    out_shape = [jax.ShapeDtypeStruct((count, width), jnp.bfloat16)] * 2
    hot_units = weights[3 if bring else 4].shape[0]
    scratch = [
        pltpu.VMEM((2 * count, width), jnp.bfloat16),
        pltpu.VMEM((2 * count, units), jnp.bfloat16),
        pltpu.VMEM((2 * count, hot_units), jnp.bfloat16),
    ]
    body = functools.partial(work_body, slots=slots, hots=hots)
    if bring:
        body = functools.partial(load_body, slots=slots, hots=hots, hot_parts=len(weights) - 4)
        shapes = [w.shape for w in weights[:3]] + [(2 * hot_units, width), (hot_units, width)]
        out_shape += [jax.ShapeDtypeStruct(shape, jnp.bfloat16) for shape in shapes]
        scratch += [pltpu.SemaphoreType.DMA((len(weights) + 2 * (units // tile_of(units, 256)) - 2,))]
    return pl.pallas_call(
        body,
        in_specs=[pl.BlockSpec(memory_space=pltpu.SMEM)] + [whole] * 2 + [far if bring else whole] * len(weights),
        out_specs=[whole] * len(out_shape),
        out_shape=out_shape,
        scratch_shapes=scratch,
        compiler_params=pltpu.CompilerParams(vmem_limit_bytes=24 << 20),
        cost_estimate=pl.CostEstimate(
            flops=2 * 2 * count * width * 3 * (units + hot_units),
            bytes_accessed=2 * 4 * count * width,
            transcendentals=2 * count * units,
        ),
    )(me, mine, shared, *(in_place(weights) if bring else weights))


def shards(tokens, w_gate, w_up, w_down, hot_gate, hot_up, hot_down, cold_routes, hot_pick, gates):
    devices = lax.axis_size("expert")
    micros, held, width = tokens.shape
    hots, _, hot_units = hot_gate.shape
    chips = devices // 2
    around, across = ring_tables(devices)
    me = lax.axis_index("expert").astype(jnp.int32).reshape(1)

    def swap(x):
        return lax.ppermute(x, "expert", across)

    def onward(x):
        return lax.ppermute(x, "expert", around)

    rows = build_rows(tokens, cold_routes, hot_pick, gates)
    flat = [jnp.swapaxes(w, 1, 2).reshape(hots * hot_units, width) for w in (hot_gate, hot_up, hot_down)]
    hot_in = flat[:2] if hots * hot_units % 16 == 0 else [jnp.concatenate(flat[:2])]
    weights = (w_gate[0], w_up[0], w_down[0], flat[2], *hot_in)
    slots = gates.shape[-1]

    own = work(me, rows, swap(rows), weights, slots, hots, bring=True)
    own, weights = own[:2], own[2:]
    coming, total = None, None
    mine = rows
    for step in range(1, chips):
        mine = onward(mine)
        if step == 1:
            mine, own = lax.optimization_barrier((mine, own))
        if total is not None:
            me, total = lax.optimization_barrier((me, total))
            coming = onward(total)
            total = None
        kept, given = work(me, mine, swap(mine), weights, slots, hots)
        if step >= chips - SPLIT:
            taken = swap(given)
            parts = coming if isinstance(coming, list) else [coming] * 2
            coming = [onward(add_half(kept, taken, before, half)) for half, before in enumerate(parts)]
            continue
        total = kept.astype(jnp.float32) + swap(given).astype(jnp.float32)
        if coming is not None:
            total = total + coming.astype(jnp.float32)
        total = total.astype(jnp.bfloat16)
    taken = swap(own[1])
    halves = [add_half(own[0], taken, before, half) for half, before in enumerate(coming)]
    return jnp.concatenate(halves).reshape(micros, held, width)


def add_body(kept, taken, before, out, *, half):
    size = out.shape[0]
    cut = slice(half * size, (half + 1) * size)
    came = cut if before.shape[0] > size else slice(None)
    total = kept[cut].astype(jnp.float32) + taken[cut].astype(jnp.float32) + before[came].astype(jnp.float32)
    out[...] = total.astype(out.dtype)


def add_half(kept, taken, before, half):
    size, width = kept.shape[0] // 2, kept.shape[1]
    near = pl.BlockSpec(memory_space=pltpu.VMEM)
    return pl.pallas_call(
        functools.partial(add_body, half=half),
        in_specs=[near] * 3,
        out_specs=near,
        out_shape=jax.ShapeDtypeStruct((size, width), kept.dtype),
        compiler_params=pltpu.CompilerParams(vmem_limit_bytes=8 << 20),
        cost_estimate=pl.CostEstimate(flops=0, bytes_accessed=(16 if half == 0 else 2) * size * width, transcendentals=0),
    )(kept, taken, before)


def solution(mesh):
    in_specs = (
        P(None, ("groups", "expert"), None),
        P("expert", None, None),
        P("expert", None, None),
        P("expert", None, None),
        P(None, None, "expert"),
        P(None, None, "expert"),
        P(None, None, "expert"),
        P(None, ("groups", "expert"), None),
        P(None, ("groups", "expert")),
        P(None, ("groups", "expert"), None),
    )
    out_specs = P(None, ("groups", "expert"), None)
    return jax.shard_map(shards, mesh=mesh, in_specs=in_specs, out_specs=out_specs, check_vma=False)
```

```python
import functools

import jax
import jax.numpy as jnp
from jax import lax
from jax.experimental import pallas as pl
from jax.experimental.pallas import tpu as pltpu
from jax.sharding import PartitionSpec as P

LANES = 128
SPLIT = 1


def ring_tables(devices):
    chips = devices // 2
    ring = list(range(0, chips, 2)) + list(range(chips - 1, 0, -2))
    around = []
    for place in range(chips):
        following, preceding = ring[(place + 1) % chips], ring[place - 1]
        around.append((2 * ring[place], 2 * following))
        around.append((2 * ring[place] + 1, 2 * preceding + 1))
    across = [(device, device ^ 1) for device in range(devices)]
    return around, across


def tile_of(size, most):
    tile = most
    while size % tile:
        tile //= 2
    return tile


def silu(value):
    return value / (1.0 + jnp.exp(-value))


def rows_body(tokens, gates, routes, pick, out, tokens_in, gates_in, routes_in, pick_in, columns, done, *, micros):
    held, width = tokens.shape[1:]
    count, slots = micros * held, gates.shape[1]
    group = 4 * slots
    depth = count * group // LANES
    pairs = [(gates, gates_in), (routes, routes_in), (pick, pick_in)]
    pairs += [(tokens.at[micro], tokens_in.at[pl.ds(micro * held, held)]) for micro in range(micros)]
    copies = [pltpu.make_async_copy(*pair, done.at[number]) for number, pair in enumerate(pairs)]
    for copy in copies:
        copy.start()
    for copy in copies[:3]:
        copy.wait()
    for micro in range(micros):
        rest = gates_in[micro]
        pieces = []
        for _ in range(3):
            pieces.append(rest.astype(jnp.bfloat16).astype(jnp.float32))
            rest = rest - pieces[-1]
        for part in range(held // depth):
            start = (micro * (held // depth) + part) * group
            cut = slice(part * depth, (part + 1) * depth)
            for k in range(slots - 1):
                columns[start + k : start + k + 1] = routes_in[k, micro : micro + 1, cut].astype(jnp.float32)
            columns[start + slots - 1 : start + slots] = pick_in[micro : micro + 1, cut].astype(jnp.float32)
            for number, piece in enumerate(pieces):
                columns[start + (number + 1) * slots : start + (number + 2) * slots] = piece[:, cut]
    out[width // LANES * count :] = columns[...].T.astype(jnp.bfloat16)
    for copy in copies[3:]:
        copy.wait()
    for block in range(width // LANES):
        out[block * count : (block + 1) * count] = tokens_in[:, block * LANES : (block + 1) * LANES]


def in_place(arrays):
    return [pltpu.with_memory_space_constraint(array, pltpu.HBM) for array in arrays]


def build_rows(tokens, cold_routes, hot_pick, gates):
    micros, held, width = tokens.shape
    slots, count = gates.shape[-1], micros * held
    depth = count * 4 * slots // LANES
    return pl.pallas_call(
        functools.partial(rows_body, micros=micros),
        in_specs=[pl.BlockSpec(memory_space=pltpu.HBM)] * 4,
        out_specs=pl.BlockSpec(memory_space=pltpu.VMEM),
        out_shape=jax.ShapeDtypeStruct((width // LANES * count + depth, LANES), jnp.bfloat16),
        scratch_shapes=[
            pltpu.VMEM((count, width), jnp.bfloat16),
            pltpu.VMEM((micros, slots, held), jnp.float32),
            pltpu.VMEM((slots - 1, micros, held), jnp.int32),
            pltpu.VMEM((micros, held), jnp.int32),
            pltpu.VMEM((LANES, depth), jnp.float32),
            pltpu.SemaphoreType.DMA((3 + micros,)),
        ],
        compiler_params=pltpu.CompilerParams(vmem_limit_bytes=8 << 20),
        cost_estimate=pl.CostEstimate(flops=0, bytes_accessed=4 * micros * held * width, transcendentals=0),
    )(*in_place([tokens, jnp.swapaxes(gates, 1, 2), jnp.transpose(cold_routes, (2, 0, 1)), hot_pick]))


def load_body(me_ref, *refs, slots, hots, hot_parts):
    blocks, refs = refs[:2], refs[2:]
    far, refs = refs[: 4 + hot_parts], refs[4 + hot_parts :]
    outs, near, scratch, done = refs[:2], refs[2:7], refs[7:10], refs[10]
    copies, offset = [[], [], [], []], 0

    def add(group, source, target):
        number = sum(len(waiting) for waiting in copies)
        copies[group].append(pltpu.make_async_copy(source, target, done.at[number]))

    for part in far[4:]:
        add(0, part, near[3].at[pl.ds(offset, part.shape[0])])
        offset += part.shape[0]
    units = near[0].shape[1]
    tile = tile_of(units, 256)
    for start in range(0, units, tile):
        for source, target in zip(far[:2], near[:2]):
            add(1, source.at[:, pl.ds(start, tile)], target.at[:, pl.ds(start, tile)])
    add(2, far[2], near[2])
    add(3, far[3], near[4])
    for group in copies:
        for copy in group:
            copy.start()

    def ready(group, number):
        if group == 1:
            copies[1][2 * number].wait()
            copies[1][2 * number + 1].wait()
            return
        for copy in copies[group]:
            copy.wait()

    work_body(me_ref, *blocks, *near, *outs, *scratch, slots=slots, hots=hots, ready=ready)


def work_body(me_ref, *refs, slots, hots, ready=lambda group, number: None):
    blocks, refs = refs[:2], refs[2:]
    (gate, up, down, hot_in, hot_out), (y_mine, y_shared), (rows, hidden, hot_hidden) = refs[:5], refs[5:7], refs[7:]
    count, width = y_mine.shape
    units = gate.shape[1]
    group = 4 * slots
    facts = []
    for number, block in enumerate(blocks):
        for column in range(width // LANES):
            place = slice(column * LANES, (column + 1) * LANES)
            rows[number * count : (number + 1) * count, place] = block[column * count : (column + 1) * count]
        packed = block[width // LANES * count :].astype(jnp.float32)
        facts += [pltpu.roll(packed, (LANES - start) % LANES, 1) if start else packed for start in range(0, LANES, group)]
    facts = jnp.concatenate(facts, axis=0)
    lane = lax.broadcasted_iota(jnp.int32, facts.shape, 1)
    named = (facts == me_ref[0].astype(jnp.float32)) & (lane < slots - 1)
    pieces = [pltpu.roll(facts, LANES - slots * number - 1, 1) for number in (1, 2, 3)]
    cold_weight = jnp.sum(jnp.where(named, pieces[0] + pieces[1] + pieces[2], 0.0), axis=1, keepdims=True)
    is_hot = (lane == slots) | (lane == 2 * slots) | (lane == 3 * slots)
    hot_weight = jnp.sum(jnp.where(is_hot, facts, 0.0), axis=1, keepdims=True)
    hot_pick = jnp.sum(jnp.where(lane == slots - 1, facts, 0.0), axis=1, keepdims=True)

    split = hot_in.shape[0] // 2
    ready(0, 0)
    both = lax.dot_general(
        rows[...], hot_in[...], (((1,), (1,)), ((), ())), preferred_element_type=jnp.float32
    )
    value = silu(both[:, :split]) * both[:, split:]
    owner = lax.broadcasted_iota(jnp.int32, value.shape, 1) // (split // hots)
    hot_hidden[...] = jnp.where(owner.astype(jnp.float32) == hot_pick, value, 0.0).astype(jnp.bfloat16)

    tile = tile_of(units, 256)
    for start in range(0, units, tile):
        cut = slice(start, start + tile)
        ready(1, start // tile)
        a = jnp.dot(rows[...], gate[:, cut], preferred_element_type=jnp.float32)
        b = jnp.dot(rows[...], up[:, cut], preferred_element_type=jnp.float32)
        hidden[:, cut] = (silu(a) * b).astype(jnp.bfloat16)
    ready(2, 0)
    ready(3, 0)
    tile = tile_of(width, 512)
    for start in range(0, width, tile):
        cut = slice(start, start + tile)
        y = cold_weight * jnp.dot(hidden[...], down[:, cut], preferred_element_type=jnp.float32)
        y = y + hot_weight * jnp.dot(hot_hidden[...], hot_out[:, cut], preferred_element_type=jnp.float32)
        y_mine[:, cut] = y[:count].astype(y_mine.dtype)
        y_shared[:, cut] = y[count:].astype(y_shared.dtype)


def work(me, mine, shared, weights, slots, hots, bring=False):
    width, units = weights[0].shape
    count = mine.shape[0] * LANES // (width + 4 * slots)
    whole, far = pl.BlockSpec(memory_space=pltpu.VMEM), pl.BlockSpec(memory_space=pltpu.HBM)
    out_shape = [jax.ShapeDtypeStruct((count, width), jnp.bfloat16)] * 2
    hot_units = weights[3 if bring else 4].shape[0]
    scratch = [
        pltpu.VMEM((2 * count, width), jnp.bfloat16),
        pltpu.VMEM((2 * count, units), jnp.bfloat16),
        pltpu.VMEM((2 * count, hot_units), jnp.bfloat16),
    ]
    body = functools.partial(work_body, slots=slots, hots=hots)
    if bring:
        body = functools.partial(load_body, slots=slots, hots=hots, hot_parts=len(weights) - 4)
        shapes = [w.shape for w in weights[:3]] + [(2 * hot_units, width), (hot_units, width)]
        out_shape += [jax.ShapeDtypeStruct(shape, jnp.bfloat16) for shape in shapes]
        scratch += [pltpu.SemaphoreType.DMA((len(weights) + 2 * (units // tile_of(units, 256)) - 2,))]
    return pl.pallas_call(
        body,
        in_specs=[pl.BlockSpec(memory_space=pltpu.SMEM)] + [whole] * 2 + [far if bring else whole] * len(weights),
        out_specs=[whole] * len(out_shape),
        out_shape=out_shape,
        scratch_shapes=scratch,
        compiler_params=pltpu.CompilerParams(vmem_limit_bytes=24 << 20),
        cost_estimate=pl.CostEstimate(
            flops=2 * 2 * count * width * 3 * (units + hot_units),
            bytes_accessed=2 * 4 * count * width,
            transcendentals=2 * count * units,
        ),
    )(me, mine, shared, *(in_place(weights) if bring else weights))


def shards(tokens, w_gate, w_up, w_down, hot_gate, hot_up, hot_down, cold_routes, hot_pick, gates):
    devices = lax.axis_size("expert")
    micros, held, width = tokens.shape
    hots, _, hot_units = hot_gate.shape
    chips = devices // 2
    around, across = ring_tables(devices)
    me = lax.axis_index("expert").astype(jnp.int32).reshape(1)

    def swap(x):
        return lax.ppermute(x, "expert", across)

    def onward(x):
        return lax.ppermute(x, "expert", around)

    rows = build_rows(tokens, cold_routes, hot_pick, gates)
    flat = [jnp.swapaxes(w, 1, 2).reshape(hots * hot_units, width) for w in (hot_gate, hot_up, hot_down)]
    hot_in = flat[:2] if hots * hot_units % 16 == 0 else [jnp.concatenate(flat[:2])]
    weights = (w_gate[0], w_up[0], w_down[0], flat[2], *hot_in)
    slots = gates.shape[-1]

    own = work(me, rows, swap(rows), weights, slots, hots, bring=True)
    own, weights = own[:2], own[2:]
    coming, total = None, None
    mine = rows
    for step in range(1, chips):
        mine = onward(mine)
        if step == 1:
            mine, own = lax.optimization_barrier((mine, own))
        if total is not None:
            me, total = lax.optimization_barrier((me, total))
            coming = onward(total)
            total = None
        kept, given = work(me, mine, swap(mine), weights, slots, hots)
        if step >= chips - SPLIT:
            taken = swap(given)
            parts = coming if isinstance(coming, list) else [coming] * 2
            coming = [onward(add_half(kept, taken, before, half)) for half, before in enumerate(parts)]
            continue
        total = kept.astype(jnp.float32) + swap(given).astype(jnp.float32)
        if coming is not None:
            total = total + coming.astype(jnp.float32)
        total = total.astype(jnp.bfloat16)
    taken = swap(own[1])
    first = add_half(own[0], taken, coming[0], 0)
    size = first.shape[0]
    second = own[0][size:].astype(jnp.float32) + taken[size:].astype(jnp.float32) + coming[1].astype(jnp.float32)
    return jnp.concatenate([first, second.astype(jnp.bfloat16)]).reshape(micros, held, width)


def add_body(kept, taken, before, out, *, half):
    size = out.shape[0]
    cut = slice(half * size, (half + 1) * size)
    came = cut if before.shape[0] > size else slice(None)
    total = kept[cut].astype(jnp.float32) + taken[cut].astype(jnp.float32) + before[came].astype(jnp.float32)
    out[...] = total.astype(out.dtype)


def add_half(kept, taken, before, half):
    size, width = kept.shape[0] // 2, kept.shape[1]
    near = pl.BlockSpec(memory_space=pltpu.VMEM)
    return pl.pallas_call(
        functools.partial(add_body, half=half),
        in_specs=[near] * 3,
        out_specs=near,
        out_shape=jax.ShapeDtypeStruct((size, width), kept.dtype),
        compiler_params=pltpu.CompilerParams(vmem_limit_bytes=8 << 20),
        cost_estimate=pl.CostEstimate(flops=0, bytes_accessed=(16 if half == 0 else 2) * size * width, transcendentals=0),
    )(kept, taken, before)


def solution(mesh):
    in_specs = (
        P(None, ("groups", "expert"), None),
        P("expert", None, None),
        P("expert", None, None),
        P("expert", None, None),
        P(None, None, "expert"),
        P(None, None, "expert"),
        P(None, None, "expert"),
        P(None, ("groups", "expert"), None),
        P(None, ("groups", "expert")),
        P(None, ("groups", "expert"), None),
    )
    out_specs = P(None, ("groups", "expert"), None)
    return jax.shard_map(shards, mesh=mesh, in_specs=in_specs, out_specs=out_specs, check_vma=False)
```
